32 devices in a mesh: section: 2 (over core), dp: 4 (over y, x), tensor: 4 (over z).
Axes of the slice: x: 2, y: 2, z: 4, core: 2. Of those that a mesh axis runs over, the one named last changes fastest.
Arguments:
- stack_ends: bfloat16 [2, 8, 1024, 1152], P('section', 'dp', 'tensor'), may hold values from -6 to 6
- cond: bfloat16 [8, 1152], P('dp'), may hold values from -6 to 6
- qkv_weight: bfloat16 [2, 1152, 3, 1152], P('section', 'dp', None, 'tensor'), may hold values from -0.1875 to 0.1875
- out_weight: bfloat16 [2, 1152, 1152], P('section', 'tensor', 'dp'), may hold values from -0.5 to 0.5
- up_weight: bfloat16 [2, 1152, 4608], P('section', 'dp', 'tensor'), may hold values from -0.1875 to 0.1875
- down_weight: bfloat16 [2, 4608, 1152], P('section', 'tensor', 'dp'), may hold values from -0.09375 to 0.09375
- adaln_weight: bfloat16 [2, 1152, 6912], P('section', 'dp', 'tensor'), may hold values from -0.1875 to 0.1875
- qv_bias: bfloat16 [2, 2, 1152], P('section'), may hold values from -2 to 2
- out_bias: bfloat16 [2, 1152], P('section'), may hold values from -2 to 2
- up_bias: bfloat16 [2, 4608], P('section'), may hold values from -2 to 2
- down_bias: bfloat16 [2, 1152], P('section'), may hold values from -2 to 2
- adaln_bias: bfloat16 [2, 6912], P('section'), may hold values from -2 to 2
Outputs:
- result_ends: float32 [2, 8, 1024, 1152], P('section', 'dp', 'tensor')
- cond_grad: float32 [8, 1152], P('dp')
- qkv_grad: float32 [2, 1152, 3, 1152], P('section', 'dp', None, 'tensor')
- out_grad: float32 [2, 1152, 1152], P('section', 'tensor', 'dp')
- up_grad: float32 [2, 1152, 4608], P('section', 'dp', 'tensor')
- down_grad: float32 [2, 4608, 1152], P('section', 'tensor', 'dp')
- adaln_grad: float32 [2, 1152, 6912], P('section', 'dp', 'tensor')
- qv_bias_grad: float32 [2, 2, 1152], P('section')
- out_bias_grad: float32 [2, 1152], P('section')
- up_bias_grad: float32 [2, 4608], P('section')
- down_bias_grad: float32 [2, 1152], P('section')
- adaln_bias_grad: float32 [2, 6912], P('section')
The draws below stay inside these ranges and needn't reach their ends.
All inputs are finite; a program needn't handle non-finite values.
Results may differ from the reference program's by a relative error of at most 0.019.
Values may be sent and summed in bfloat16 or wider, within the bound.
A program may use at most 256 MiB of HBM per device.

```python
import math
import jax
import jax.numpy as jnp
from jax import lax

D = 1152
HEADS = 16
HD = 72
FF = 4608
SEQ = 1024
LAT_DEV = 2
LAT = 8


def steps_of(stream_key, extent, shards, least, high):
    def one(axis_at, parts):
        steps = jax.random.uniform(jax.random.fold_in(jax.random.fold_in(stream_key, 6), axis_at), (parts,), jnp.float32, least / len(shards), high / len(shards))
        return jnp.repeat(jnp.exp(steps), extent[axis_at] // parts).reshape((-1,) + (1,) * (len(extent) - axis_at - 1))

    level = one(*shards[0])
    for cut in shards[1:]:
        level = level * one(*cut)
    return level


def scatter_about(own_key, shape, width, most, cuts=(), held_as=jnp.bfloat16):
    drawn = width * jax.random.normal(own_key, shape, jnp.float32)
    if cuts:
        drawn = drawn * steps_of(own_key, shape, cuts, -0.22, 0.18)
    return jnp.clip(drawn, -most, most).astype(held_as)


def setup_inputs(seed: int = 0) -> dict:
    streams_of = jax.random.split(jax.random.key(seed), 13)
    return {
        "stack_ends": scatter_about(streams_of[0], (2, LAT, SEQ, D), 1.0, 6.0, ((0, 2), (1, 4), (2, 4))),
        "cond": scatter_about(streams_of[1], (LAT, D), 1.0, 6.0, ((0, 4),)),
        "qkv_weight": scatter_about(streams_of[2], (2, D, 3, D), D ** -0.5, 0.1875, ((0, 2), (1, 4), (3, 4))),
        "out_weight": scatter_about(streams_of[3], (2, D, D), (D // 8) ** -0.5, 0.5, ((0, 2), (1, 4), (2, 4))),
        "up_weight": scatter_about(streams_of[4], (2, D, FF), D ** -0.5, 0.1875, ((0, 2), (1, 4), (2, 4))),
        "down_weight": scatter_about(streams_of[5], (2, FF, D), FF ** -0.5, 0.09375, ((0, 2), (1, 4), (2, 4))),
        "adaln_weight": scatter_about(streams_of[6], (2, D, 6 * D), D ** -0.5, 0.1875, ((0, 2), (1, 4), (2, 4))),
        "qv_bias": scatter_about(streams_of[7], (2, 2, D), 0.3, 2.0, ((0, 2),)),
        "out_bias": scatter_about(streams_of[8], (2, D), 0.3, 2.0, ((0, 2),)),
        "up_bias": scatter_about(streams_of[9], (2, FF), 0.3, 2.0, ((0, 2),)),
        "down_bias": scatter_about(streams_of[10], (2, D), 0.3, 2.0, ((0, 2),)),
        "adaln_bias": scatter_about(streams_of[11], (2, 6 * D), 0.3, 2.0, ((0, 2),)),
    }


highest = lax.Precision.HIGHEST
norm_eps = 1e-06

@jax.custom_vjp
def low(v):
    return lax.optimization_barrier(v.astype(jnp.bfloat16)).astype(jnp.float32)

@jax.custom_vjp
def low_back(v):
    return v

def low_keep(v):
    return (low(v), None)

def low_pass(kept, grad):
    return (grad,)

def back_keep(v):
    return (v, None)

def back_low(kept, grad):
    return (low(grad),)
low.defvjp(low_keep, low_pass)
low_back.defvjp(back_keep, back_low)

def layer_norm(values):
    centred = values - lax.optimization_barrier(jnp.mean(values, axis=-1, keepdims=True))
    variance = lax.optimization_barrier(jnp.mean(centred * centred, axis=-1, keepdims=True))
    return centred * lax.rsqrt(variance + norm_eps)

def product(left, right):
    return jnp.dot(left, right, precision=highest, preferred_element_type=jnp.float32)

def one_latent(triple):
    queries, keys_in, values_in = triple
    scores = jnp.einsum('qhe,khe->hqk', queries, keys_in, precision=highest) * (1.0 / math.sqrt(HD))
    scores = low_back(scores)
    weights_soft = low(jax.nn.softmax(scores, axis=-1))
    return jnp.einsum('hqk,khe->qhe', weights_soft, values_in, precision=highest)

def block(inputs, silu_low, params):
    w_qkv, w_out, w_up, w_down, w_ada, b_qv, b_out, b_up, b_down, b_ada = params
    groups, length = (inputs.shape[0], inputs.shape[1])
    modulation = low_back(product(silu_low, w_ada) + b_ada)
    pieces = [modulation[:, None, part * D:(part + 1) * D] for part in range(6)]
    shift_attn, scale_attn, gate_attn, shift_mlp, scale_mlp, gate_mlp = pieces
    normed = low(layer_norm(inputs) * (1.0 + scale_attn) + shift_attn).reshape(groups * length, D)
    projected = product(normed, w_qkv.reshape(D, 3 * D)).reshape(groups, length, 3, D)
    queries = low(low_back(projected[:, :, 0] + b_qv[0]))
    keys_all = low(low_back(projected[:, :, 1]))
    values_all = low(low_back(projected[:, :, 2] + b_qv[1]))
    shaped = tuple((member.reshape(groups, length, HEADS, HD) for member in (queries, keys_all, values_all)))
    attended = lax.map(jax.checkpoint(one_latent), shaped)
    attended = low(low_back(attended.reshape(groups * length, D)))
    branch_attn = low_back(product(attended, w_out) + b_out).reshape(groups, length, D)
    middle = inputs + gate_attn * branch_attn
    normed_mlp = low(layer_norm(middle) * (1.0 + scale_mlp) + shift_mlp).reshape(groups * length, D)
    hidden_pre = low_back(product(normed_mlp, w_up) + b_up)
    hidden = low(jax.nn.gelu(hidden_pre, approximate=True))
    branch_mlp = low_back(product(hidden, w_down) + b_down).reshape(groups, length, D)
    return middle + gate_mlp * branch_mlp

def reference(stack_ends, cond, qkv_weight, out_weight, up_weight, down_weight, adaln_weight, qv_bias, out_bias, up_bias, down_bias, adaln_bias):
    weights_all = tuple((member.astype(jnp.float32) for member in (qkv_weight, out_weight, up_weight, down_weight, adaln_weight, qv_bias, out_bias, up_bias, down_bias, adaln_bias)))
    group_count = LAT // LAT_DEV
    inputs = stack_ends[0].astype(jnp.float32).reshape(group_count, LAT_DEV, SEQ, D)
    cotangent = stack_ends[1].astype(jnp.float32).reshape(group_count, LAT_DEV, SEQ, D)
    conds = cond.astype(jnp.float32).reshape(group_count, LAT_DEV, D)

    def stacked(block_in, cond_in, weights_in):
        silu_low = low(jax.nn.silu(cond_in))
        first = tuple((member[0] for member in weights_in))
        second = tuple((member[1] for member in weights_in))
        boundary = low(low_back(block(block_in, silu_low, first)))
        return block(boundary, silu_low, second)

    def one_group(totals, group_item):
        block_in, cond_in, cot_in = group_item
        result, pullback = jax.vjp(stacked, block_in, cond_in, weights_all)
        grad_in, grad_cond, grad_weights = pullback(cot_in)
        totals = jax.tree.map(lambda left, right: left + right, totals, grad_weights)
        return (totals, (result, grad_in, grad_cond))
    zero_grads = jax.tree.map(jnp.zeros_like, weights_all)
    totals, (results, grads_in, grads_cond) = lax.scan(one_group, zero_grads, (inputs, conds, cotangent))
    result_ends = jnp.stack([grads_in.reshape(LAT, SEQ, D), results.reshape(LAT, SEQ, D)])
    return (result_ends, grads_cond.reshape(LAT, D), totals[0], totals[1], totals[2], totals[3], totals[4], totals[5], totals[6], totals[7], totals[8], totals[9])
```

```python
import math

import jax
import jax.numpy as jnp
from jax import lax
from jax.sharding import PartitionSpec as P

HD = 72
norm_eps = 1e-06
SWAP = [(0, 1), (1, 0)]
SCALE = 1.0 / math.sqrt(HD)


def norm_parts(values):
    centred = values - jnp.mean(values, axis=-1, keepdims=True)
    inverse = lax.rsqrt(jnp.mean(centred * centred, axis=-1, keepdims=True) + norm_eps)
    return centred * inverse, inverse


def norm_back(normal, inverse, grad):
    pulled = grad - jnp.mean(grad, axis=-1, keepdims=True)
    return (pulled - normal * jnp.mean(grad * normal, axis=-1, keepdims=True)) * inverse


def gelu_tanh(values):
    return jax.nn.gelu(values, approximate=True)


def spread(values):
    return lax.all_gather(values, "tensor", axis=0, tiled=True)


def collect(values):
    return lax.psum_scatter(
        values.astype(jnp.bfloat16), "tensor", scatter_dimension=0, tiled=True
    ).astype(jnp.float32)


def mm(left, right, left_dim, right_dim):
    return lax.dot_general(
        left, right, (((left_dim,), (right_dim,)), ((), ())), preferred_element_type=jnp.float32
    )


def heads_first(rows):
    return rows.reshape(rows.shape[0], -1, HD).transpose(1, 0, 2)


def heads_side(heads):
    return heads.transpose(1, 0, 2).reshape(heads.shape[1], -1)


def forward(inputs, modulation, w_attn, w_mlp, biases):
    b_qkv, b_out, b_up, b_down = biases
    shift_attn, scale_attn, gate_attn, shift_mlp, scale_mlp, gate_mlp = modulation
    cols = w_attn.shape[1] // 4
    units = w_mlp.shape[1] // 2
    norm_in, inv_in = norm_parts(inputs)
    normed = spread((norm_in * (1.0 + scale_attn) + shift_attn).astype(jnp.bfloat16))
    projected = (mm(normed, w_attn[:, : 3 * cols], 1, 0) + b_qkv).astype(jnp.bfloat16)
    queries, keys, values = [
        heads_first(projected[:, part * cols : (part + 1) * cols]) for part in range(3)
    ]
    scores = jnp.einsum("hqe,hke->hqk", queries, keys, preferred_element_type=jnp.float32) * SCALE
    probs = jax.nn.softmax(scores, axis=-1).astype(jnp.bfloat16)
    attended = jnp.einsum("hqk,hke->hqe", probs, values, preferred_element_type=jnp.float32)
    attended = attended.astype(jnp.bfloat16)
    attended_rows = heads_side(attended)
    branch_attn = collect(mm(attended_rows, w_attn[:, 3 * cols :], 1, 1)) + b_out
    middle = inputs + gate_attn * branch_attn
    norm_mid, inv_mid = norm_parts(middle)
    normed_mlp = spread((norm_mid * (1.0 + scale_mlp) + shift_mlp).astype(jnp.bfloat16))
    hidden_pre = mm(normed_mlp, w_mlp[:, :units], 1, 0) + b_up
    hidden = gelu_tanh(hidden_pre).astype(jnp.bfloat16)
    branch_mlp = collect(mm(hidden, w_mlp[:, units:], 1, 1)) + b_down
    outputs = middle + gate_mlp * branch_mlp
    stored = (
        norm_in, inv_in, normed, queries, keys, values, probs, attended, attended_rows,
        branch_attn, norm_mid, inv_mid, normed_mlp, hidden_pre, hidden, branch_mlp,
    )
    return outputs, stored


def backward(upstream, stored, modulation, w_attn, w_mlp):
    (
        norm_in, inv_in, normed, queries, keys, values, probs, attended, attended_rows,
        branch_attn, norm_mid, inv_mid, normed_mlp, hidden_pre, hidden, branch_mlp,
    ) = stored
    shift_attn, scale_attn, gate_attn, shift_mlp, scale_mlp, gate_mlp = modulation
    cols = w_attn.shape[1] // 4
    units = w_mlp.shape[1] // 2
    grad_gate_mlp = jnp.sum(upstream * branch_mlp, axis=0)
    grad_branch = (gate_mlp * upstream).astype(jnp.bfloat16)
    bias_down = jnp.sum(grad_branch.astype(jnp.float32), axis=0)
    grad_rows = spread(grad_branch)
    grad_hidden = mm(grad_rows, w_mlp[:, units:], 1, 0)
    _, gelu_pull = jax.vjp(gelu_tanh, hidden_pre)
    grad_pre = gelu_pull(grad_hidden)[0].astype(jnp.bfloat16)
    grad_normed = collect(mm(grad_pre, w_mlp[:, :units], 1, 1))
    bias_up = jnp.sum(grad_pre.astype(jnp.float32), axis=0)
    mlp_grads = jnp.concatenate(
        [
            mm(normed_mlp, grad_pre, 0, 0).astype(jnp.bfloat16),
            mm(grad_rows, hidden, 0, 0).astype(jnp.bfloat16),
        ],
        axis=1,
    )
    grad_shift_mlp = jnp.sum(grad_normed, axis=0)
    grad_scale_mlp = jnp.sum(grad_normed * norm_mid, axis=0)
    grad_middle = upstream + norm_back(norm_mid, inv_mid, grad_normed * (1.0 + scale_mlp))
    grad_gate_attn = jnp.sum(grad_middle * branch_attn, axis=0)
    grad_branch = (gate_attn * grad_middle).astype(jnp.bfloat16)
    bias_out = jnp.sum(grad_branch.astype(jnp.float32), axis=0)
    grad_rows = spread(grad_branch)
    grad_attended = heads_first(mm(grad_rows, w_attn[:, 3 * cols :], 1, 0).astype(jnp.bfloat16))
    row_sums = jnp.sum(
        grad_attended.astype(jnp.float32) * attended.astype(jnp.float32), axis=-1, keepdims=True
    )
    grad_probs = jnp.einsum(
        "hqe,hke->hqk", grad_attended, values, preferred_element_type=jnp.float32
    )
    grad_scores = (probs.astype(jnp.float32) * (grad_probs - row_sums)).astype(jnp.bfloat16)
    grad_values = jnp.einsum(
        "hqk,hqe->hke", probs, grad_attended, preferred_element_type=jnp.float32
    )
    grad_queries = SCALE * jnp.einsum(
        "hqk,hke->hqe", grad_scores, keys, preferred_element_type=jnp.float32
    )
    grad_keys = SCALE * jnp.einsum(
        "hqk,hqe->hke", grad_scores, queries, preferred_element_type=jnp.float32
    )
    grad_proj = jnp.concatenate(
        [
            heads_side(member.astype(jnp.bfloat16))
            for member in (grad_queries, grad_keys, grad_values)
        ],
        axis=1,
    )
    grad_normed = collect(mm(grad_proj, w_attn[:, : 3 * cols], 1, 1))
    bias_qkv = jnp.sum(grad_proj.astype(jnp.float32), axis=0)
    attn_grads = jnp.concatenate(
        [
            mm(normed, grad_proj, 0, 0).astype(jnp.bfloat16),
            mm(grad_rows, attended_rows, 0, 0).astype(jnp.bfloat16),
        ],
        axis=1,
    )
    grad_shift_attn = jnp.sum(grad_normed, axis=0)
    grad_scale_attn = jnp.sum(grad_normed * norm_in, axis=0)
    grad_inputs = grad_middle + norm_back(norm_in, inv_in, grad_normed * (1.0 + scale_attn))
    mod_terms = jnp.concatenate(
        [
            grad_shift_attn, grad_scale_attn, grad_gate_attn,
            grad_shift_mlp, grad_scale_mlp, grad_gate_mlp,
        ]
    )
    bias_grads = (bias_qkv[:cols], bias_qkv[2 * cols :], bias_out, bias_up, bias_down)
    return grad_inputs, attn_grads, mlp_grads, bias_grads, mod_terms


def on_device(
    stack_ends,
    cond,
    qkv_weight,
    out_weight,
    up_weight,
    down_weight,
    adaln_weight,
    qv_bias,
    out_bias,
    up_bias,
    down_bias,
    adaln_bias,
):
    section_rank = lax.axis_index("section")
    tensor_rank = lax.axis_index("tensor")
    dp_rank = lax.axis_index("dp")
    is_first = section_rank == 0
    width = stack_ends.shape[3]
    depth = qkv_weight.shape[1]
    cols = qkv_weight.shape[3]
    units = up_weight.shape[2]
    mod_cols = adaln_weight.shape[2]
    lat_here = cond.shape[0]
    lat_all = lat_here * lax.axis_size("dp")

    def swap(value):
        return lax.ppermute(value, "section", SWAP)

    def by_block(own, other):
        return (jnp.where(is_first, own, other), jnp.where(is_first, other, own))

    own_ends = stack_ends[0]
    mine = lax.dynamic_index_in_dim(own_ends, section_rank, 0, keepdims=False)
    theirs = swap(lax.dynamic_index_in_dim(own_ends, 1 - section_rank, 0, keepdims=False))
    inputs, cotangent = by_block(mine, theirs)

    cond_all = lax.all_gather(cond, "dp", axis=0, tiled=True).astype(jnp.float32)
    silu_all = jax.nn.silu(cond_all).astype(jnp.bfloat16)
    silu_rows = lax.dynamic_slice_in_dim(silu_all, dp_rank * depth, depth, 1)
    mod_part = lax.psum_scatter(
        mm(silu_rows, adaln_weight[0], 1, 0), "dp", scatter_dimension=0, tiled=True
    )
    mod_all = lax.all_gather(mod_part, ("section", "tensor"), axis=0)
    mod_own = lax.dynamic_index_in_dim(mod_all, section_rank, 1, keepdims=False)
    mod_own = mod_own.reshape(2, -1)

    attn_own = lax.all_gather(
        jnp.concatenate([qkv_weight[0].reshape(depth, 3 * cols), out_weight[0].T], axis=1),
        "dp", axis=0, tiled=True,
    )
    attn_blocks = by_block(attn_own, swap(attn_own))
    mlp_own = lax.all_gather(
        jnp.concatenate([up_weight[0], down_weight[0].T], axis=1), "dp", axis=0, tiled=True
    )
    mlp_blocks = by_block(mlp_own, swap(mlp_own))

    bias_flat = jnp.concatenate(
        [qv_bias[0].reshape(-1), out_bias[0], up_bias[0], down_bias[0], adaln_bias[0]]
    )
    bias_blocks = by_block(bias_flat, swap(bias_flat))
    sizes = (width, width, width, up_bias.shape[1], width, adaln_bias.shape[1])
    marks = [0]
    for size in sizes:
        marks.append(marks[-1] + size)

    modulations = []
    biases = []
    for block in range(2):
        parts = [
            bias_blocks[block][marks[k] : marks[k + 1]].astype(jnp.float32) for k in range(6)
        ]

        def cut(vector, size):
            return lax.dynamic_slice_in_dim(vector, tensor_rank * size, size, 0)

        b_qkv = jnp.concatenate(
            [cut(parts[0], cols), jnp.zeros((cols,), jnp.float32), cut(parts[1], cols)]
        )
        biases.append((b_qkv, parts[2], cut(parts[3], units), parts[4]))
        whole = (mod_own[block] + parts[5]).reshape(6, 1, width)
        modulations.append([whole[k] for k in range(6)])

    boundary, stored_first = forward(
        inputs.astype(jnp.float32), modulations[0], attn_blocks[0], mlp_blocks[0], biases[0]
    )
    boundary = boundary.astype(jnp.bfloat16).astype(jnp.float32)
    outputs, stored_last = forward(
        boundary, modulations[1], attn_blocks[1], mlp_blocks[1], biases[1]
    )
    back_last = backward(
        cotangent.astype(jnp.float32), stored_last, modulations[1], attn_blocks[1], mlp_blocks[1]
    )
    upstream = back_last[0].astype(jnp.bfloat16).astype(jnp.float32)
    back_first = backward(
        upstream, stored_first, modulations[0], attn_blocks[0], mlp_blocks[0]
    )
    backs = (back_first, back_last)

    def settle(which):
        kept = jnp.where(is_first, backs[0][which], backs[1][which])
        sent = swap(jnp.where(is_first, backs[1][which], backs[0][which]))
        total = (kept.astype(jnp.float32) + sent.astype(jnp.float32)).astype(jnp.bfloat16)
        return lax.psum_scatter(total, "dp", scatter_dimension=0, tiled=True).astype(jnp.float32)

    mlp_total = settle(2)
    attn_total = settle(1)

    first_end, last_end = back_first[0], outputs
    kept = jnp.where(is_first, first_end, last_end)
    sent = swap(jnp.where(is_first, last_end, first_end))
    result_ends = jnp.stack(by_block(kept, sent))[None]

    mod_terms = lax.psum_scatter(
        jnp.stack([backs[0][4], backs[1][4]]), "tensor", scatter_dimension=1, tiled=True
    )
    mod_grads = lax.all_gather(mod_terms, ("dp", "section"), axis=0)
    mod_grads = lax.dynamic_index_in_dim(mod_grads, section_rank, 1, keepdims=False)
    mod_grads = mod_grads.astype(jnp.bfloat16)
    grad_ada = mm(silu_rows, mod_grads, 0, 0)
    bias_ada = jnp.sum(mod_grads.astype(jnp.float32), axis=0)
    grad_silu = mm(mod_grads, adaln_weight[0], 1, 1)

    def place(vector, size, rank):
        return lax.dynamic_update_slice_in_dim(
            jnp.zeros((size,), jnp.float32), vector, rank * vector.shape[0], 0
        )

    pieces = []
    for block in range(2):
        bias_q, bias_v, bias_out, bias_up, bias_down = backs[block][3]
        share = jnp.where((section_rank == block) & (dp_rank == 0), bias_ada, 0.0)
        pieces += [
            place(bias_q, width, tensor_rank),
            place(bias_v, width, tensor_rank),
            bias_out,
            place(bias_up, sizes[3], tensor_rank),
            bias_down,
            place(share, sizes[5], tensor_rank),
        ]
    pieces.append(
        lax.dynamic_update_slice_in_dim(
            jnp.zeros((lat_all, width), jnp.float32), grad_silu, dp_rank * depth, 1
        ).reshape(-1)
    )
    summed = lax.psum(jnp.concatenate(pieces), ("section", "dp", "tensor"))
    per_block = marks[-1]
    bias_sums = jnp.where(is_first, summed[:per_block], summed[per_block : 2 * per_block])
    silu_total = summed[2 * per_block :].reshape(lat_all, width)
    silu_total = lax.dynamic_slice_in_dim(silu_total, dp_rank * lat_here, lat_here, 0)
    _, silu_pull = jax.vjp(jax.nn.silu, cond.astype(jnp.float32))
    cond_grad = silu_pull(silu_total)[0]
    return (
        result_ends,
        cond_grad,
        attn_total[:, : 3 * cols].reshape(1, depth, 3, cols),
        attn_total[:, 3 * cols :].T[None],
        mlp_total[:, :units][None],
        mlp_total[:, units:].T[None],
        grad_ada[None],
        bias_sums[: marks[2]].reshape(1, 2, width),
        bias_sums[marks[2] : marks[3]][None],
        bias_sums[marks[3] : marks[4]][None],
        bias_sums[marks[4] : marks[5]][None],
        bias_sums[marks[5] :][None],
    )


def solution(mesh):
    in_specs = (
        P("section", "dp", "tensor", None),
        P("dp", None),
        P("section", "dp", None, "tensor"),
        P("section", "tensor", "dp"),
        P("section", "dp", "tensor"),
        P("section", "tensor", "dp"),
        P("section", "dp", "tensor"),
        P("section", None, None),
        P("section", None),
        P("section", None),
        P("section", None),
        P("section", None),
    )
    out_specs = (
        P("section", "dp", "tensor", None),
        P("dp", None),
        P("section", "dp", None, "tensor"),
        P("section", "tensor", "dp"),
        P("section", "dp", "tensor"),
        P("section", "tensor", "dp"),
        P("section", "dp", "tensor"),
        P("section", None, None),
        P("section", None),
        P("section", None),
        P("section", None),
        P("section", None),
    )
    return jax.shard_map(
        on_device, mesh=mesh, in_specs=in_specs, out_specs=out_specs, check_vma=False
    )
```

```python
import functools
import math

import jax
import jax.numpy as jnp
from jax import lax
from jax.experimental import pallas as pl
from jax.experimental.pallas import tpu as pltpu
from jax.sharding import Mesh
from jax.sharding import PartitionSpec as P

HD = 72
norm_eps = 1e-06
SWAP = [(0, 1), (1, 0)]
SCALE = 1.0 / math.sqrt(HD)


def norm_parts(values):
    centred = values - jnp.mean(values, axis=-1, keepdims=True)
    inverse = lax.rsqrt(jnp.mean(centred * centred, axis=-1, keepdims=True) + norm_eps)
    return centred * inverse, inverse


def norm_back(normal, inverse, grad):
    pulled = grad - jnp.mean(grad, axis=-1, keepdims=True)
    return (pulled - normal * jnp.mean(grad * normal, axis=-1, keepdims=True)) * inverse


def gelu_tanh(values):
    return jax.nn.gelu(values, approximate=True)


MESH = pl.DeviceIdType.MESH
CHUNKS = 2


def greet(nz, side, place):
    barrier = pltpu.get_barrier_semaphore()
    pl.semaphore_signal(barrier, inc=1, device_id={"section": 1 - side}, device_id_type=MESH)
    for j in range(1, nz):
        pl.semaphore_signal(
            barrier, inc=1, device_id={"zl": lax.rem(place + j, nz)}, device_id_type=MESH
        )
    pl.semaphore_wait(barrier, nz)


def push(src, dst, send, recv, target):
    return pltpu.make_async_remote_copy(
        src_ref=src, dst_ref=dst, send_sem=send, recv_sem=recv,
        device_id=target, device_id_type=MESH,
    )


def spread_kernel(nz, x_ref, out_ref, local, send_c, recv_c, send_z, recv_z, send_f, recv_f):
    side = lax.axis_index("section")
    place = lax.axis_index("zl")
    own = side * nz + place
    step = x_ref.shape[0] // CHUNKS
    greet(nz, side, place)
    along = []
    for c in range(CHUNKS):
        rows = pl.ds(c * step, step)
        for j in range(1, nz):
            copy = push(
                x_ref.at[rows], out_ref.at[own, rows], send_z.at[c, j - 1], recv_z.at[c, j - 1],
                {"zl": lax.rem(place + j, nz)},
            )
            copy.start()
            along.append(copy)
    across = push(x_ref, out_ref.at[own], send_c, recv_c, {"section": 1 - side})
    across.start()
    kept = pltpu.make_async_copy(x_ref, out_ref.at[own], local)
    kept.start()
    handed = []
    for c in range(CHUNKS):
        rows = pl.ds(c * step, step)
        for j in range(1, nz):
            along[c * (nz - 1) + j - 1].wait_recv()
            came = side * nz + lax.rem(place - j + nz, nz)
            copy = push(
                out_ref.at[came, rows], out_ref.at[came, rows],
                send_f.at[c, j - 1], recv_f.at[c, j - 1], {"section": 1 - side},
            )
            copy.start()
            handed.append(copy)
    kept.wait()
    across.wait()
    for copy in along:
        copy.wait_send()
    for copy in handed:
        copy.wait()


def spread(values):
    nz = lax.axis_size("zl")
    many = (CHUNKS, nz - 1)
    dma = pltpu.SemaphoreType.DMA
    gathered = pl.pallas_call(
        functools.partial(spread_kernel, nz),
        out_shape=jax.ShapeDtypeStruct((2 * nz,) + values.shape, values.dtype),
        in_specs=[pl.BlockSpec(memory_space=pl.ANY)],
        out_specs=pl.BlockSpec(memory_space=pl.ANY),
        scratch_shapes=[dma, dma, dma, dma(many), dma(many), dma(many), dma(many)],
        compiler_params=pltpu.CompilerParams(collective_id=0, has_side_effects=True),
        name="spread_tokens",
    )(values)
    return gathered.reshape(-1, values.shape[1])


def collect_kernel(
    nz, x_ref, out_ref, core_buf, mid_buf, z_buf, send_c, recv_c, send_z, recv_z
):
    side = lax.axis_index("section")
    place = lax.axis_index("zl")
    step = x_ref.shape[1] // CHUNKS
    greet(nz, side, place)
    across = {}
    for j in list(range(1, nz)) + [0]:
        there = lax.rem(place + j, nz)
        for c in range(CHUNKS):
            rows = pl.ds(c * step, step)
            copy = push(
                x_ref.at[(1 - side) * nz + there, rows], core_buf.at[j, rows],
                send_c.at[c, j], recv_c.at[c, j], {"section": 1 - side},
            )
            copy.start()
            across[c, j] = copy
    along = {}
    for j in range(1, nz):
        there = lax.rem(place + j, nz)
        for c in range(CHUNKS):
            rows = pl.ds(c * step, step)
            across[c, j].wait_recv()
            mid_buf[j - 1, rows] = (
                x_ref[side * nz + there, rows].astype(jnp.float32)
                + core_buf[j, rows].astype(jnp.float32)
            ).astype(jnp.bfloat16)
            copy = push(
                mid_buf.at[j - 1, rows], z_buf.at[j - 1, rows],
                send_z.at[c, j - 1], recv_z.at[c, j - 1], {"zl": there},
            )
            copy.start()
            along[c, j] = copy
    for c in range(CHUNKS):
        rows = pl.ds(c * step, step)
        across[c, 0].wait_recv()
        total = x_ref[side * nz + place, rows].astype(jnp.float32) + core_buf[0, rows].astype(
            jnp.float32
        )
        for j in range(1, nz):
            along[c, j].wait_recv()
            total = total + z_buf[j - 1, rows].astype(jnp.float32)
        out_ref[rows] = total
    for copy in across.values():
        copy.wait_send()
    for copy in along.values():
        copy.wait_send()


def collect(values):
    nz = lax.axis_size("zl")
    width = values.shape[1]
    rows = values.shape[0] // (2 * nz)
    dma = pltpu.SemaphoreType.DMA
    vmem = pl.BlockSpec(memory_space=pltpu.VMEM)
    return pl.pallas_call(
        functools.partial(collect_kernel, nz),
        out_shape=jax.ShapeDtypeStruct((rows, width), jnp.float32),
        in_specs=[vmem],
        out_specs=vmem,
        scratch_shapes=[
            pltpu.VMEM((nz, rows, width), jnp.bfloat16),
            pltpu.VMEM((nz - 1, rows, width), jnp.bfloat16),
            pltpu.VMEM((nz - 1, rows, width), jnp.bfloat16),
            dma((CHUNKS, nz)),
            dma((CHUNKS, nz)),
            dma((CHUNKS, nz - 1)),
            dma((CHUNKS, nz - 1)),
        ],
        compiler_params=pltpu.CompilerParams(
            collective_id=1, has_side_effects=True, vmem_limit_bytes=24 * 2**20
        ),
        name="collect_tokens",
    )(values.astype(jnp.bfloat16).reshape(2 * nz, rows, width))


def mm(left, right, left_dim, right_dim):
    return lax.dot_general(
        left, right, (((left_dim,), (right_dim,)), ((), ())), preferred_element_type=jnp.float32
    )


def heads_first(rows):
    return rows.reshape(rows.shape[0], -1, HD).transpose(1, 0, 2)


def heads_side(heads):
    return heads.transpose(1, 0, 2).reshape(heads.shape[1], -1)


def forward(inputs, modulation, w_attn, w_mlp, biases):
    b_qkv, b_out, b_up, b_down = biases
    shift_attn, scale_attn, gate_attn, shift_mlp, scale_mlp, gate_mlp = modulation
    cols = w_attn.shape[1] // 4
    units = w_mlp.shape[1] // 2
    norm_in, inv_in = norm_parts(inputs)
    normed = spread((norm_in * (1.0 + scale_attn) + shift_attn).astype(jnp.bfloat16))
    projected = (mm(normed, w_attn[:, : 3 * cols], 1, 0) + b_qkv).astype(jnp.bfloat16)
    queries, keys, values = [
        heads_first(projected[:, part * cols : (part + 1) * cols]) for part in range(3)
    ]
    scores = jnp.einsum("hqe,hke->hqk", queries, keys, preferred_element_type=jnp.float32) * SCALE
    probs = jax.nn.softmax(scores, axis=-1).astype(jnp.bfloat16)
    attended = jnp.einsum("hqk,hke->hqe", probs, values, preferred_element_type=jnp.float32)
    attended = attended.astype(jnp.bfloat16)
    attended_rows = heads_side(attended)
    branch_attn = collect(mm(attended_rows, w_attn[:, 3 * cols :], 1, 1)) + b_out
    middle = inputs + gate_attn * branch_attn
    norm_mid, inv_mid = norm_parts(middle)
    normed_mlp = spread((norm_mid * (1.0 + scale_mlp) + shift_mlp).astype(jnp.bfloat16))
    hidden_pre = mm(normed_mlp, w_mlp[:, :units], 1, 0) + b_up
    hidden = gelu_tanh(hidden_pre).astype(jnp.bfloat16)
    branch_mlp = collect(mm(hidden, w_mlp[:, units:], 1, 1)) + b_down
    outputs = middle + gate_mlp * branch_mlp
    stored = (
        norm_in, inv_in, normed, queries, keys, values, probs, attended, attended_rows,
        branch_attn, norm_mid, inv_mid, normed_mlp, hidden_pre, hidden, branch_mlp,
    )
    return outputs, stored


def scatter_dp(grads):
    return lax.psum_scatter(grads, "dp", scatter_dimension=0, tiled=True)


def backward(upstream, stored, modulation, w_attn, w_mlp, before):
    (
        norm_in, inv_in, normed, queries, keys, values, probs, attended, attended_rows,
        branch_attn, norm_mid, inv_mid, normed_mlp, hidden_pre, hidden, branch_mlp,
    ) = stored
    shift_attn, scale_attn, gate_attn, shift_mlp, scale_mlp, gate_mlp = modulation
    cols = w_attn.shape[1] // 4
    units = w_mlp.shape[1] // 2
    grad_gate_mlp = jnp.sum(upstream * branch_mlp, axis=0)
    grad_branch = (gate_mlp * upstream).astype(jnp.bfloat16)
    bias_down = jnp.sum(grad_branch.astype(jnp.float32), axis=0)
    grad_rows = spread(grad_branch)
    grad_hidden = mm(grad_rows, w_mlp[:, units:], 1, 0)
    _, gelu_pull = jax.vjp(gelu_tanh, hidden_pre)
    grad_pre = gelu_pull(grad_hidden)[0].astype(jnp.bfloat16)
    grad_normed = collect(mm(grad_pre, w_mlp[:, :units], 1, 1))
    bias_up = jnp.sum(grad_pre.astype(jnp.float32), axis=0)
    mlp_grads = jnp.concatenate(
        [
            mm(normed_mlp, grad_pre, 0, 0).astype(jnp.bfloat16),
            mm(grad_rows, hidden, 0, 0).astype(jnp.bfloat16),
        ],
        axis=1,
    )
    if before is not None:
        grad_normed, before = lax.optimization_barrier((grad_normed, before))
    mlp_grads = scatter_dp(mlp_grads)
    grad_shift_mlp = jnp.sum(grad_normed, axis=0)
    grad_scale_mlp = jnp.sum(grad_normed * norm_mid, axis=0)
    grad_middle = upstream + norm_back(norm_mid, inv_mid, grad_normed * (1.0 + scale_mlp))
    grad_gate_attn = jnp.sum(grad_middle * branch_attn, axis=0)
    grad_branch = (gate_attn * grad_middle).astype(jnp.bfloat16)
    bias_out = jnp.sum(grad_branch.astype(jnp.float32), axis=0)
    grad_rows = spread(grad_branch)
    grad_attended = heads_first(mm(grad_rows, w_attn[:, 3 * cols :], 1, 0).astype(jnp.bfloat16))
    row_sums = jnp.sum(
        grad_attended.astype(jnp.float32) * attended.astype(jnp.float32), axis=-1, keepdims=True
    )
    grad_probs = jnp.einsum(
        "hqe,hke->hqk", grad_attended, values, preferred_element_type=jnp.float32
    )
    grad_scores = (probs.astype(jnp.float32) * (grad_probs - row_sums)).astype(jnp.bfloat16)
    grad_values = jnp.einsum(
        "hqk,hqe->hke", probs, grad_attended, preferred_element_type=jnp.float32
    )
    grad_queries = SCALE * jnp.einsum(
        "hqk,hke->hqe", grad_scores, keys, preferred_element_type=jnp.float32
    )
    grad_keys = SCALE * jnp.einsum(
        "hqk,hqe->hke", grad_scores, queries, preferred_element_type=jnp.float32
    )
    grad_proj = jnp.concatenate(
        [
            heads_side(member.astype(jnp.bfloat16))
            for member in (grad_queries, grad_keys, grad_values)
        ],
        axis=1,
    )
    grad_normed = collect(mm(grad_proj, w_attn[:, : 3 * cols], 1, 1))
    bias_qkv = jnp.sum(grad_proj.astype(jnp.float32), axis=0)
    attn_grads = jnp.concatenate(
        [
            mm(normed, grad_proj, 0, 0).astype(jnp.bfloat16),
            mm(grad_rows, attended_rows, 0, 0).astype(jnp.bfloat16),
        ],
        axis=1,
    )
    grad_normed, mlp_grads = lax.optimization_barrier((grad_normed, mlp_grads))
    attn_grads = scatter_dp(attn_grads)
    grad_shift_attn = jnp.sum(grad_normed, axis=0)
    grad_scale_attn = jnp.sum(grad_normed * norm_in, axis=0)
    grad_inputs = grad_middle + norm_back(norm_in, inv_in, grad_normed * (1.0 + scale_attn))
    mod_terms = jnp.concatenate(
        [
            grad_shift_attn, grad_scale_attn, grad_gate_attn,
            grad_shift_mlp, grad_scale_mlp, grad_gate_mlp,
        ]
    )
    bias_grads = (bias_qkv[:cols], bias_qkv[2 * cols :], bias_out, bias_up, bias_down)
    return grad_inputs, attn_grads, mlp_grads, bias_grads, mod_terms, before


def on_device(
    stack_ends,
    cond,
    qkv_weight,
    out_weight,
    up_weight,
    down_weight,
    adaln_weight,
    qv_bias,
    out_bias,
    up_bias,
    down_bias,
    adaln_bias,
):
    section_rank = lax.axis_index("section")
    half_rank = lax.axis_index("zh")
    halves = lax.axis_size("zl")
    tensor_rank = half_rank * halves + lax.axis_index("zl")
    part_rank = section_rank * halves + lax.axis_index("zl")
    at_home = section_rank == half_rank
    dp_rank = lax.axis_index("dp")
    is_first = section_rank == 0
    width = stack_ends.shape[3]
    depth = qkv_weight.shape[1]
    cols = qkv_weight.shape[3]
    units = up_weight.shape[2]
    mod_cols = adaln_weight.shape[2]
    lat_here = cond.shape[0]
    lat_all = lat_here * lax.axis_size("dp")

    def swap(value):
        return lax.ppermute(value, "section", SWAP)

    def by_block(own, other):
        return (jnp.where(is_first, own, other), jnp.where(is_first, other, own))

    def bring(own):
        pair = jnp.stack(by_block(own, swap(own)))
        return pair, lax.ppermute(pair, ("section", "zh"), [(0, 1), (3, 2)])

    def fetch(own):
        pair, moved = bring(own)
        return jnp.where(at_home, pair, moved)

    ends = jnp.stack(by_block(stack_ends[0], swap(stack_ends[0])))
    mine = lax.dynamic_index_in_dim(ends, half_rank, 1, keepdims=False)
    theirs = lax.ppermute(
        lax.dynamic_index_in_dim(ends, 1 - half_rank, 1, keepdims=False),
        ("section", "zh"), [(0, 1), (3, 2)],
    )
    inputs, cotangent = jnp.where(at_home, mine, theirs)

    cond_all = lax.all_gather(cond, "dp", axis=0, tiled=True).astype(jnp.float32)
    silu_all = jax.nn.silu(cond_all).astype(jnp.bfloat16)
    silu_rows = lax.dynamic_slice_in_dim(silu_all, dp_rank * depth, depth, 1)
    mod_part = lax.psum_scatter(
        mm(silu_rows, adaln_weight[0], 1, 0), "dp", scatter_dimension=0, tiled=True
    )
    mod_all = lax.all_gather(mod_part, ("section", "zh", "zl"), axis=0)
    mod_own = lax.dynamic_index_in_dim(mod_all, half_rank, 1, keepdims=False)
    mod_own = mod_own.reshape(2, -1)

    attn_pair = fetch(
        jnp.concatenate([qkv_weight[0].reshape(depth, 3 * cols), out_weight[0].T], axis=1)
    )
    mlp_pair = fetch(jnp.concatenate([up_weight[0], down_weight[0].T], axis=1))
    attn_blocks = []
    mlp_blocks = []
    for block in range(2):
        attn_blocks.append(lax.all_gather(attn_pair[block], "dp", axis=0, tiled=True))
        mlp_blocks.append(lax.all_gather(mlp_pair[block], "dp", axis=0, tiled=True))

    bias_flat = jnp.concatenate(
        [qv_bias[0].reshape(-1), out_bias[0], up_bias[0], down_bias[0], adaln_bias[0]]
    )
    bias_blocks = by_block(bias_flat, swap(bias_flat))
    sizes = (width, width, width, up_bias.shape[1], width, adaln_bias.shape[1])
    marks = [0]
    for size in sizes:
        marks.append(marks[-1] + size)

    modulations = []
    biases = []
    for block in range(2):
        parts = [
            bias_blocks[block][marks[k] : marks[k + 1]].astype(jnp.float32) for k in range(6)
        ]

        def cut(vector, size):
            return lax.dynamic_slice_in_dim(vector, part_rank * size, size, 0)

        b_qkv = jnp.concatenate(
            [cut(parts[0], cols), jnp.zeros((cols,), jnp.float32), cut(parts[1], cols)]
        )
        biases.append((b_qkv, parts[2], cut(parts[3], units), parts[4]))
        whole = (mod_own[block] + parts[5]).reshape(6, 1, width)
        modulations.append([whole[k] for k in range(6)])

    boundary, stored_first = forward(
        inputs.astype(jnp.float32), modulations[0], attn_blocks[0], mlp_blocks[0], biases[0]
    )
    boundary = boundary.astype(jnp.bfloat16).astype(jnp.float32)
    outputs, stored_last = forward(
        boundary, modulations[1], attn_blocks[1], mlp_blocks[1], biases[1]
    )
    back_last = backward(
        cotangent.astype(jnp.float32), stored_last, modulations[1], attn_blocks[1], mlp_blocks[1], None
    )
    upstream = back_last[0].astype(jnp.bfloat16).astype(jnp.float32)
    back_first = backward(
        upstream, stored_first, modulations[0], attn_blocks[0], mlp_blocks[0], back_last[1]
    )
    back_last = (back_last[0], back_first[5]) + back_last[2:]
    backs = (back_first, back_last)

    def settle(which):
        pair = jnp.stack([back[which] for back in backs])
        moved = lax.ppermute(pair, ("section", "zh"), [(1, 0), (2, 3)])
        total = pair.astype(jnp.float32) + moved.astype(jnp.float32)
        kept = lax.dynamic_index_in_dim(total, section_rank, 0, keepdims=False)
        sent = lax.dynamic_index_in_dim(total, 1 - section_rank, 0, keepdims=False)
        sent = swap(sent.astype(jnp.bfloat16)).astype(jnp.float32)
        return jnp.where(at_home, kept, sent)

    mlp_total = settle(2)
    attn_total = settle(1)

    ends = jnp.stack([back_first[0], outputs])
    moved = lax.ppermute(ends.astype(jnp.bfloat16), ("section", "zh"), [(1, 0), (2, 3)])
    moved = moved.astype(jnp.float32)
    latents = [
        jnp.where(half_rank == lat, ends, moved)
        for lat in range(2)
    ]
    ends = jnp.stack(latents, axis=1)
    kept = lax.dynamic_index_in_dim(ends, section_rank, 0, keepdims=False)
    sent = swap(lax.dynamic_index_in_dim(ends, 1 - section_rank, 0, keepdims=False))
    result_ends = jnp.where(at_home, kept, sent)[None]

    mod_terms = jnp.stack([backs[0][4], backs[1][4]])
    mod_terms = jnp.stack(
        [jnp.where(half_rank == lat, mod_terms, 0.0) for lat in range(2)]
    ).reshape(2, -1, mod_cols).transpose(1, 0, 2)
    mod_terms = lax.psum_scatter(
        mod_terms.reshape(-1, 2 * mod_cols), ("section", "zh", "zl"), scatter_dimension=0, tiled=True
    ).reshape(2, mod_cols)
    mod_grads = lax.all_gather(mod_terms, "dp", axis=0, tiled=True)
    mod_grads = mod_grads.astype(jnp.bfloat16)
    grad_ada = mm(silu_rows, mod_grads, 0, 0)
    bias_ada = jnp.sum(mod_grads.astype(jnp.float32), axis=0)
    grad_silu = mm(mod_grads, adaln_weight[0], 1, 1)

    def place(vector, size, rank):
        return lax.dynamic_update_slice_in_dim(
            jnp.zeros((size,), jnp.float32), vector, rank * vector.shape[0], 0
        )

    pieces = []
    for block in range(2):
        bias_q, bias_v, bias_out, bias_up, bias_down = backs[block][3]
        share = jnp.where((section_rank == block) & (dp_rank == 0), bias_ada, 0.0)
        pieces += [
            place(bias_q, width, part_rank),
            place(bias_v, width, part_rank),
            bias_out,
            place(bias_up, sizes[3], part_rank),
            bias_down,
            place(share, sizes[5], tensor_rank),
        ]
    pieces.append(
        lax.dynamic_update_slice_in_dim(
            jnp.zeros((lat_all, width), jnp.float32), grad_silu, dp_rank * depth, 1
        ).reshape(-1)
    )
    summed = lax.psum(jnp.concatenate(pieces), ("section", "dp", "zh", "zl"))
    per_block = marks[-1]
    bias_sums = jnp.where(is_first, summed[:per_block], summed[per_block : 2 * per_block])
    silu_total = summed[2 * per_block :].reshape(lat_all, width)
    silu_total = lax.dynamic_slice_in_dim(silu_total, dp_rank * lat_here, lat_here, 0)
    _, silu_pull = jax.vjp(jax.nn.silu, cond.astype(jnp.float32))
    cond_grad = silu_pull(silu_total)[0]
    return (
        result_ends,
        cond_grad,
        attn_total[:, : 3 * cols].reshape(1, depth, 3, cols),
        attn_total[:, 3 * cols :].T[None],
        mlp_total[:, :units][None],
        mlp_total[:, units:].T[None],
        grad_ada[None],
        bias_sums[: marks[2]].reshape(1, 2, width),
        bias_sums[marks[2] : marks[3]][None],
        bias_sums[marks[3] : marks[4]][None],
        bias_sums[marks[4] : marks[5]][None],
        bias_sums[marks[5] :][None],
    )


def solution(mesh):
    section, dp, tensor = mesh.devices.shape
    fine = Mesh(mesh.devices.reshape(section, dp, 2, tensor // 2), ("section", "dp", "zh", "zl"))
    in_specs = (
        P("section", "dp", ("zh", "zl"), None),
        P("dp", None),
        P("section", "dp", None, ("zh", "zl")),
        P("section", ("zh", "zl"), "dp"),
        P("section", "dp", ("zh", "zl")),
        P("section", ("zh", "zl"), "dp"),
        P("section", "dp", ("zh", "zl")),
        P("section", None, None),
        P("section", None),
        P("section", None),
        P("section", None),
        P("section", None),
    )
    out_specs = (
        P("section", "dp", ("zh", "zl"), None),
        P("dp", None),
        P("section", "dp", None, ("zh", "zl")),
        P("section", ("zh", "zl"), "dp"),
        P("section", "dp", ("zh", "zl")),
        P("section", ("zh", "zl"), "dp"),
        P("section", "dp", ("zh", "zl")),
        P("section", None, None),
        P("section", None),
        P("section", None),
        P("section", None),
        P("section", None),
    )
    return jax.shard_map(
        on_device, mesh=fine, in_specs=in_specs, out_specs=out_specs, check_vma=False
    )
```
